32 devices in a mesh: blk: 8 (over z, core), lat: 4 (over y, x).
Axes of the slice: x: 2, y: 2, z: 4, core: 2. Of those that a mesh axis runs over, the one named last changes fastest.
Arguments:
- displacement: float32 [2, 3, 318240], P(None, None, ('blk', 'lat')), may hold values from -5 to 5, as said below
- velocity: float32 [2, 3, 318240], P(None, None, ('blk', 'lat')), may hold values from -2.5 to 2.5, as said below
- lumped_mass: float32 [318240], P(('blk', 'lat')), may hold values from 0.25 to 225, as said below
- shear_modulus: float32 [125, 4096], P(None, ('blk', 'lat')), may hold values from 0.3 to 1
- lame_modulus: float32 [125, 4096], P(None, ('blk', 'lat')), may hold values from 0.3 to 1
- adjoint_sources: bfloat16 [32, 3, 318240], P(None, None, ('blk', 'lat')), may hold values from -24 to 24
- node_numbers: int32 [125, 4096], P(None, ('blk', 'lat')), may hold values from 0 to 9944, as said below
- event_frequency: int32 [2, 32], replicated, may hold values from 0 to 31, each once within a row
Outputs:
- final_displacement: float32 [2, 3, 318240], P(None, None, ('blk', 'lat'))
- final_velocity: float32 [2, 3, 318240], P(None, None, ('blk', 'lat'))
- strain_spectrum: float32 [2, 32, 2, 5, 4096], P(None, None, None, None, ('blk', 'lat'))
The draws below stay inside these ranges and needn't reach their ends.
Inputs may be any that keep to these rules, and one draw needn't show every extreme that they name: `node_numbers`: each device's columns number its 9945 nodes, each node once across its elements' shared points. A device's element at grid place (ex, ey, ez), 0 <= ex < 2, 0 <= ey < 4, 0 <= ez < 16, touches a neighbour's face when ex or ey is at an end of its range; the first 128 columns of each device are these elements in the order of ex * 4 * 16 + ey * 16 + ez, the remaining columns the other elements in the same order. `event_frequency`: each row gives the events of one supershot distinct frequencies. `displacement`: all copies of a mesh node hold equal values. `velocity`: all copies of a mesh node hold equal values. `lumped_mass`: all copies of a mesh node hold equal values, the mass assembled over all elements of the mesh.
All inputs are finite; a program needn't handle non-finite values.
Results may differ from the reference program's by a relative error of at most 0.0034.
Values sent between devices are 32-bit elements; how exact they have to be, the bound alone decides.
A program may use at most 128 MiB of HBM per device.

```python
import math
import jax
import jax.numpy as jnp
import numpy as np
from jax import lax

EXB = 2
EYL = 4
EZ = 16
SHOTS = 2
NFREQ = 32
STEP_TOTAL = 4
NODES_EL = 125
EVENTS = 32
NXN = 9
NYN = 17
NZN = 65
NODES_DEV = 9945
ELEMS = 128
FACE_B = 1105
FACE_L = 585
NODES = 318240
ELEMS_ALL = 4096
N_BLK = 8
N_LAT = 4


def layout_tables(key):
    base = jax.random.fold_in(key, 4242)
    devices = N_BLK * N_LAT
    number_keys = jax.random.split(jax.random.fold_in(base, 1), devices)
    numbering = jax.vmap(lambda single: jax.random.permutation(single, NODES_DEV))(number_keys).astype(jnp.int32)
    elements = jnp.arange(ELEMS, dtype=jnp.int32)
    along = elements // (EYL * EZ)
    across = elements // EZ % EYL
    inner = ((along > 0) & (along < EXB - 1) & (across > 0) & (across < EYL - 1)).astype(jnp.int32)
    scores = inner * ELEMS + elements
    single_order = jnp.argsort(scores).astype(jnp.int32)
    order = jnp.broadcast_to(single_order[None, :], (devices, ELEMS))
    return (numbering, order)


def global_index(numbering):
    devices = N_BLK * N_LAT
    cycle_span = N_BLK * (NXN - 1)
    lat_span = N_LAT * (NYN - 1) + 1
    device_ids = jnp.arange(devices, dtype=jnp.int32)
    cycle_pos = device_ids // N_LAT
    lat_pos = device_ids % N_LAT
    local = jnp.arange(NODES_DEV, dtype=jnp.int32)
    first = local // (NYN * NZN)
    second = local // NZN % NYN
    third = local % NZN
    cycle_coord = (cycle_pos[:, None] * (NXN - 1) + first[None, :]) % cycle_span
    lat_coord = lat_pos[:, None] * (NYN - 1) + second[None, :]
    structured = (cycle_coord * lat_span + lat_coord) * NZN + third[None, :]
    inverse = jnp.argsort(numbering, axis=1).astype(jnp.int32)
    return jnp.take_along_axis(structured, inverse, axis=1).reshape(-1)


def grid_total():
    return N_BLK * (NXN - 1) * (N_LAT * (NYN - 1) + 1) * NZN


def draw_displacement(key, part):
    numbering, order = layout_tables(key)
    noise_key = jax.random.fold_in(key, 11)
    values = jnp.clip(jax.random.normal(noise_key, (SHOTS * 3, grid_total()), jnp.float32), -5.0, 5.0)
    return values[:, global_index(numbering)].reshape(SHOTS, 3, -1)


def draw_velocity(key, part):
    numbering, order = layout_tables(key)
    noise_key = jax.random.fold_in(key, 12)
    values = jnp.clip(0.5 * jax.random.normal(noise_key, (SHOTS * 3, grid_total()), jnp.float32), -2.5, 2.5)
    return values[:, global_index(numbering)].reshape(SHOTS, 3, -1)


def assembled_weights(span, closed):
    table = jnp.array([0.2, 49.0 / 90.0, 32.0 / 45.0, 49.0 / 90.0], jnp.float32)
    coords = jnp.arange(span, dtype=jnp.int32)
    values = table[coords % 4]
    if closed:
        return values
    ends = (coords == 0) | (coords == span - 1)
    return jnp.where(ends, 0.1, values)


def draw_lumped_mass(key, part):
    numbering, order = layout_tables(key)
    noise_key = jax.random.fold_in(key, 13)
    cycle_span = N_BLK * (NXN - 1)
    lat_span = N_LAT * (NYN - 1) + 1
    density = jnp.exp(jax.random.uniform(noise_key, (grid_total(),), jnp.float32, jnp.log(2000.0), jnp.log(5000.0)))
    cube = assembled_weights(cycle_span, True)[:, None, None] * assembled_weights(lat_span, False)[None, :, None] * assembled_weights(NZN, False)[None, None, :] / 8.0
    mass = density * cube.reshape(-1)
    return mass[global_index(numbering)]


def draw_node_numbers(key, part):
    numbering, order = layout_tables(key)
    along = order // (EYL * EZ)
    across = order // EZ % EYL
    depth = order % EZ
    points = jnp.arange(125, dtype=jnp.int32)
    first = points // 25
    second = points // 5 % 5
    third = points % 5
    grid = ((4 * along[:, None, :] + first[None, :, None]) * NYN + 4 * across[:, None, :] + second[None, :, None]) * NZN + 4 * depth[:, None, :] + third[None, :, None]
    numbers = jax.vmap(lambda table, where: table[where])(numbering, grid)
    return numbers.transpose(1, 0, 2).reshape(125, -1).astype(jnp.int32)


def shard_levels(key, shape, shards, low, top_value):
    factor_of = 1.0
    for position, parts in shards:
        heights = jax.random.uniform(jax.random.fold_in(jax.random.fold_in(key, 6), position), (parts,), jnp.float32, low / len(shards), top_value / len(shards))
        factor_of = factor_of * jnp.repeat(jnp.exp(heights), shape[position] // parts).reshape((-1,) + (1,) * (len(shape) - 1 - position))
    return factor_of


def centred(key, extent, deviation, most, cuts=(), kind=jnp.bfloat16):
    values = jax.random.normal(key, extent, jnp.float32) * deviation
    if len(cuts) > 0:
        values = shard_levels(key, extent, cuts, -0.22, 0.18) * values
    return jnp.clip(values, min=-most, max=most).astype(kind)


def setup_inputs(seed: int = 0) -> dict:
    key_of = jax.random.split(jax.random.key(seed), 9)
    return {
        "displacement": draw_displacement(jax.random.fold_in(key_of[8], 71), 0),
        "velocity": draw_velocity(jax.random.fold_in(key_of[8], 71), 0),
        "lumped_mass": draw_lumped_mass(jax.random.fold_in(key_of[8], 71), 0),
        "shear_modulus": jnp.clip(jnp.exp(math.log(1.0) - 1.2039728 * jax.random.uniform(key_of[3], (NODES_EL, ELEMS_ALL), jnp.float32) ** shard_levels(key_of[3], (NODES_EL, ELEMS_ALL), ((1, 32),), -0.2, 0.2)), 0.3, 1.0),
        "lame_modulus": jnp.clip(jnp.exp(math.log(1.0) - 1.2039728 * jax.random.uniform(key_of[4], (NODES_EL, ELEMS_ALL), jnp.float32) ** shard_levels(key_of[4], (NODES_EL, ELEMS_ALL), ((1, 32),), -0.2, 0.2)), 0.3, 1.0),
        "adjoint_sources": centred(key_of[5], (EVENTS, 3, NODES), 4.0, 24.0, ((2, 32),)),
        "node_numbers": draw_node_numbers(jax.random.fold_in(key_of[8], 71), 0),
        "event_frequency": jax.vmap(lambda own: jax.random.permutation(own, NFREQ))(jax.random.split(key_of[7], SHOTS)).reshape((SHOTS, NFREQ)).astype(jnp.int32),
    }


highest = lax.Precision.HIGHEST

def gll_tables():
    points = np.array([-1.0, -math.sqrt(3.0 / 7.0), 0.0, math.sqrt(3.0 / 7.0), 1.0])
    weights = np.array([0.1, 49.0 / 90.0, 32.0 / 45.0, 49.0 / 90.0, 0.1])
    products = np.ones(5)
    for target in range(5):
        for source in range(5):
            if source != target:
                products[target] = products[target] * (points[target] - points[source])
    derivative = np.zeros((5, 5))
    for target in range(5):
        for source in range(5):
            if source != target:
                derivative[target, source] = products[target] / products[source] / (points[target] - points[source])
        derivative[target, target] = -np.sum(derivative[target])
    weight_cube = weights[:, None, None] * weights[None, :, None] * weights[None, None, :] / 8.0
    return (jnp.asarray(derivative, jnp.float32), jnp.asarray(weight_cube, jnp.float32))

def grid_tables():
    elements = np.arange(ELEMS)
    along = elements // (EYL * EZ)
    across = elements // EZ % EYL
    inner = ((along > 0) & (along < EXB - 1) & (across > 0) & (across < EYL - 1)).astype(np.int64)
    order = np.argsort(inner * ELEMS + elements, kind='stable')
    columns_of = np.argsort(order, kind='stable')
    nodes = np.arange(NODES_DEV)
    first = nodes // (NYN * NZN)
    second = nodes // NZN % NYN
    third = nodes % NZN
    elem_x = np.minimum(first // 4, EXB - 1)
    elem_y = np.minimum(second // 4, EYL - 1)
    elem_z = np.minimum(third // 4, EZ - 1)
    point_rows = 25 * (first - 4 * elem_x) + 5 * (second - 4 * elem_y) + (third - 4 * elem_z)
    point_cols = columns_of[(elem_x * EYL + elem_y) * EZ + elem_z]
    return (order, columns_of, point_rows, point_cols)

def face_places():
    span_b = np.arange(NYN * NZN)
    cycle_low = span_b
    cycle_high = (NXN - 1) * NYN * NZN + span_b
    span_l = np.arange(NXN * NZN)
    rows = span_l // NZN
    deep = span_l % NZN
    lat_low = rows * NYN * NZN + deep
    lat_high = (rows * NYN + NYN - 1) * NZN + deep
    return (np.stack([cycle_low, cycle_high]), np.stack([lat_low, lat_high]))

def source_terms(event_frequency):
    angular_frequencies = jnp.pi * (1.0 + jnp.arange(NFREQ, dtype=jnp.float32)) / (NFREQ + 1.0)
    onehot = (event_frequency[:, :, None] == jnp.arange(NFREQ, dtype=jnp.int32)[None, None, :]).astype(jnp.float32)
    selected_entry = lax.optimization_barrier(jnp.sum(onehot * angular_frequencies[None, None, :], axis=2))
    sample_times = 1.0 + jnp.arange(STEP_TOTAL, dtype=jnp.float32)
    source_pulse = jnp.cos(sample_times[:, None, None] * selected_entry[None, :, :])
    phase_angles = angular_frequencies[:, None] * sample_times[None, :]
    spectra = jnp.stack([jnp.cos(phase_angles), -jnp.sin(phase_angles)])
    return (source_pulse.astype(jnp.bfloat16), spectra)

def element_forces(motion, numbers, shear, lame, derivative, weight_cube):
    elem_count = numbers.shape[1]
    shot_count = motion.shape[0] // 3
    nodal = motion[:, numbers].reshape(shot_count, 3, 5, 5, 5, elem_count)
    grads = (2.0 * jnp.einsum('il,scljkn->scijkn', derivative, nodal, precision=highest), 2.0 * jnp.einsum('jl,scilkn->scijkn', derivative, nodal, precision=highest), 2.0 * jnp.einsum('kl,scijln->scijkn', derivative, nodal, precision=highest))
    shear_pts = shear.reshape(5, 5, 5, elem_count)
    lame_pts = lame.reshape(5, 5, 5, elem_count)
    trace = grads[0][:, 0] + grads[1][:, 1] + grads[2][:, 2]
    pressure = lame_pts * trace
    weighted = weight_cube[:, :, :, None]
    forms = ('il,scijkn->scljkn', 'jl,scijkn->scilkn', 'kl,scijkn->scijln')
    internal = jnp.zeros(nodal.shape, jnp.float32)
    for direction in range(3):
        pieces = []
        for strain_part in range(3):
            stress = shear_pts * (grads[direction][:, strain_part] + grads[strain_part][:, direction])
            if strain_part == direction:
                stress = stress + pressure
            pieces.append(weighted * stress)
        flux = jnp.stack(pieces, axis=1)
        internal = internal + jnp.einsum(forms[direction], derivative, flux, precision=highest)
    internal = 2.0 * internal.reshape(3 * shot_count, 125, elem_count)
    summed = jnp.zeros(motion.shape, jnp.float32).at[:, numbers].add(internal)
    third = trace / 3.0
    strains = jnp.stack([grads[0][:, 0] - third, grads[1][:, 1] - third, 0.5 * (grads[0][:, 1] + grads[1][:, 0]), 0.5 * (grads[0][:, 2] + grads[2][:, 0]), 0.5 * (grads[1][:, 2] + grads[2][:, 1])], axis=1)
    integral = jnp.einsum('sqijkn,ijk->sqn', strains, weight_cube, precision=highest)
    return (summed, integral)

def pick_faces(values, index):
    return values[:, index]

def place_faces(values, index, extra):
    return values.at[:, index].add(extra)

def assemble(balance, cycle_index, lat_index):
    devices = N_BLK * N_LAT
    components = balance.shape[1]
    pick = jax.vmap(pick_faces)
    place = jax.vmap(place_faces)
    cycle_vals = pick(balance, cycle_index).reshape(N_BLK, N_LAT, components, 2, FACE_B)
    from_lower = jnp.roll(cycle_vals[:, :, :, 1], 1, axis=0).reshape(devices, components, FACE_B)
    from_upper = jnp.roll(cycle_vals[:, :, :, 0], -1, axis=0).reshape(devices, components, FACE_B)
    balance = place(balance, cycle_index[:, 0], from_lower)
    balance = place(balance, cycle_index[:, 1], from_upper)
    lat_vals = pick(balance, lat_index).reshape(N_BLK, N_LAT, components, 2, FACE_L)
    zero_row = jnp.zeros_like(lat_vals[:, :1, :, 1])
    from_lower = jnp.concatenate([zero_row, lat_vals[:, :-1, :, 1]], axis=1).reshape(devices, components, FACE_L)
    from_upper = jnp.concatenate([lat_vals[:, 1:, :, 0], zero_row], axis=1).reshape(devices, components, FACE_L)
    balance = place(balance, lat_index[:, 0], from_lower)
    balance = place(balance, lat_index[:, 1], from_upper)
    return balance

def reference(displacement, velocity, lumped_mass, shear_modulus, lame_modulus, adjoint_sources, node_numbers, event_frequency):
    devices = N_BLK * N_LAT
    components = 3 * SHOTS
    node_count = displacement.shape[2] // devices
    elem_count = node_numbers.shape[1] // devices
    derivative, weight_cube = gll_tables()
    source_pulse, spectra = source_terms(event_frequency)
    order, columns_of, point_rows, point_cols = grid_tables()
    cycle_place, lat_place = face_places()

    def split(array, width):
        return array.reshape(array.shape[0], devices, width).transpose(1, 0, 2)
    motion = split(displacement.reshape(components, -1), node_count)
    speeds = split(velocity.reshape(components, -1), node_count)
    masses = lumped_mass.reshape(devices, 1, node_count)
    numbers = split(node_numbers, elem_count)
    shear_dev = split(shear_modulus, elem_count)
    lame_dev = split(lame_modulus, elem_count)
    grid_nodes = numbers[:, point_rows, point_cols]
    cycle_index = grid_nodes[:, cycle_place]
    lat_index = grid_nodes[:, lat_place]
    flat_sources = adjoint_sources.reshape(adjoint_sources.shape[0], -1)
    spectrum = jnp.zeros((2, NFREQ, SHOTS, 5, devices, elem_count), jnp.float32)

    def local_work(inputs):
        return element_forces(inputs[0], inputs[1], inputs[2], inputs[3], derivative, weight_cube)
    for step in range(STEP_TOTAL):
        force = jnp.dot(source_pulse[step], flat_sources, preferred_element_type=jnp.float32)
        force = split(force.reshape(components, -1), node_count)
        internal, integral = lax.map(local_work, (motion, numbers, shear_dev, lame_dev))
        balance = assemble(force - internal, cycle_index, lat_index)
        speeds = speeds + balance / masses
        spectrum = spectrum + spectra[:, :, step][:, :, None, None, None, None] * integral.transpose(1, 2, 0, 3)[None, None]
        motion = motion + speeds
    final_displacement = motion.transpose(1, 0, 2).reshape(SHOTS, 3, devices * node_count)
    final_velocity = speeds.transpose(1, 0, 2).reshape(SHOTS, 3, devices * node_count)
    return (final_displacement, final_velocity, spectrum.reshape(2, NFREQ, SHOTS, 5, devices * elem_count))
```

```python
import functools
import math

import jax
import jax.numpy as jnp
import ml_dtypes
import numpy as np
from jax import lax
from jax.experimental import pallas as pl
from jax.experimental.pallas import tpu as pltpu
from jax.sharding import PartitionSpec as P

EXB = 2
EYL = 4
EZ = 16
NFREQ = 32
STEPS = 4
ELEMS = EXB * EYL * EZ
LANES = 128
ROWS = 208
COMPS = 6
TABLE = 40
FORCE_AT = 16
HALF_X = EYL * EZ
VMEM = pltpu.VMEM
MESH = pl.DeviceIdType.MESH
LIMIT = 56 * 1024 * 1024


def row_of(a, b, c):
    return (5 * a + b) * 8 + c


def gll():
    points = np.array([-1.0, -math.sqrt(3.0 / 7.0), 0.0, math.sqrt(3.0 / 7.0), 1.0])
    weights = np.array([0.1, 49.0 / 90.0, 32.0 / 45.0, 49.0 / 90.0, 0.1])
    products = np.ones(5)
    for i in range(5):
        for j in range(5):
            if i != j:
                products[i] *= points[i] - points[j]
    derivative = np.zeros((5, 5))
    for i in range(5):
        for j in range(5):
            if i != j:
                derivative[i, j] = products[i] / products[j] / (points[i] - points[j])
        derivative[i, i] = -np.sum(derivative[i])
    cube = weights[:, None, None] * weights[None, :, None] * weights[None, None, :] / 8.0
    return derivative, cube


def operators():
    derivative, cube = gll()
    forward = np.zeros((3, ROWS, ROWS))
    weight = np.zeros((ROWS, LANES))
    for a in range(5):
        for b in range(5):
            for c in range(5):
                r = row_of(a, b, c)
                weight[r] = cube[a, b, c]
                for l in range(5):
                    forward[0, r, row_of(l, b, c)] += 2.0 * derivative[a, l]
                    forward[1, r, row_of(a, l, c)] += 2.0 * derivative[b, l]
                    forward[2, r, row_of(a, b, l)] += 2.0 * derivative[c, l]
    backward = forward.transpose(2, 0, 1).reshape(ROWS, 3 * ROWS).copy()
    for d in range(3):
        forward[d, 5] = weight[:, 0] @ forward[d]
    return forward.reshape(3 * ROWS, ROWS), backward, weight.astype(np.float32)


def two_parts(values):
    high = values.astype(np.float32).astype(ml_dtypes.bfloat16)
    low = (values - high.astype(np.float64)).astype(ml_dtypes.bfloat16)
    return jnp.asarray(high), jnp.asarray(low)


def owner_classes():
    every = list(range(ELEMS))
    out = []
    for last_a in (False, True):
        for last_b in (False, True):
            for last_c in (False, True):
                own = [
                    e
                    for e in every
                    if (not last_a or e // HALF_X == EXB - 1)
                    and (not last_b or e // EZ % EYL == EYL - 1)
                    and (not last_c or e % EZ == EZ - 1)
                ]
                out.append((last_a, last_b, last_c, own))
    return out


def over_points(body):
    for last_a, last_b, last_c, own in owner_classes():
        na, nb, nc = (1 if last_a else 4), (1 if last_b else 4), (1 if last_c else 4)

        def step(i, carry, own=own, na=na, nb=nb, nc=nc, la=last_a, lb=last_b, lc=last_c):
            a = 4 if la else i // (nb * nc)
            b = 4 if lb else (i // nc) % nb
            c = 4 if lc else i % nc
            body(25 * a + 5 * b + c, (5 * a + b) * 8 + c, own, (la, lb, lc))
            return carry

        lax.fori_loop(0, na * nb * nc, step, 0)


def lane_parts(shape):
    lane = lax.broadcasted_iota(jnp.int32, shape, len(shape) - 1)
    return lane // HALF_X, lane // EZ % EYL, lane % EZ


def gather_kernel(numbers, values, out, table, stage):
    count = values.shape[1] // LANES

    def turn(i, carry):
        at = pl.multiple_of(i * LANES, LANES)
        block = values[:, pl.ds(at, LANES)]
        full = jnp.concatenate([block, jnp.zeros((LANES - TABLE, LANES), jnp.float32)], axis=0)
        table[pl.ds(at, LANES), :] = full.T
        return carry

    lax.fori_loop(0, count, turn, 0)
    out[...] = jnp.zeros_like(out)
    stage[...] = jnp.zeros_like(stage)
    ex, ey, ez = lane_parts((TABLE, LANES))

    def point(p, row, own, last):
        for e in own:
            stage[pl.ds(e, 1), :] = table[pl.ds(numbers[p, e], 1), :]
        block = stage[...].T[:TABLE]
        keep = None
        for flag, part, top in zip(last, (ex, ey, ez), (EXB - 1, EYL - 1, EZ - 1)):
            if flag:
                keep = (part == top) if keep is None else keep & (part == top)
        if keep is not None:
            block = jnp.where(keep, block, 0.0)
        out[pl.ds(row, TABLE, stride=ROWS), :] = block

    over_points(point)


def local_sum(x):
    x = x.reshape(ROWS // 8, 8, LANES)
    sub = lax.broadcasted_iota(jnp.int32, x.shape, 1)
    ez = lax.broadcasted_iota(jnp.int32, x.shape, 2) % EZ
    turned = pltpu.roll(x, 4, 1)
    x = x + jnp.where((sub == 4) & (ez < EZ - 1), pltpu.roll(turned, LANES - 1, 2), 0.0)
    x = x + jnp.where((sub == 0) & (ez > 0), pltpu.roll(turned, 1, 2), 0.0)
    ex, ey, _ = lane_parts((8, LANES))
    blocks = [x[i] for i in range(ROWS // 8)]
    for a in range(5):
        low, high = blocks[5 * a], blocks[5 * a + 4]
        blocks[5 * a] = low + jnp.where(ey > 0, pltpu.roll(high, EZ, 1), 0.0)
        blocks[5 * a + 4] = high + jnp.where(ey < EYL - 1, pltpu.roll(low, LANES - EZ, 1), 0.0)
    for b in range(5):
        low, high = blocks[b], blocks[20 + b]
        blocks[b] = low + jnp.where(ex > 0, pltpu.roll(high, HALF_X, 1), 0.0)
        blocks[20 + b] = high + jnp.where(ex < EXB - 1, pltpu.roll(low, LANES - HALF_X, 1), 0.0)
    return jnp.concatenate(blocks, axis=0)


def parts(x):
    high = x.astype(jnp.bfloat16)
    return high, (x - high.astype(jnp.float32)).astype(jnp.bfloat16)


def product(left_high, left_low, high, low):
    dot = functools.partial(jnp.dot, preferred_element_type=jnp.float32)
    return dot(left_high, high) + dot(left_high, low) + dot(left_low, high)


def step_kernel(
    n_blk, n_lat,
    gathered, shear, lame, weight, fwd_high, fwd_low, bwd_high, bwd_low,
    state, integrals,
    u, v, force, inverse, shear_w, lame_w, grads, flux_high, flux_low, balance,
    send_x, send_y, recv_x, recv_y, sx, rx, sy, ry,
):
    blk, lat = lax.axis_index("blk"), lax.axis_index("lat")
    up, down = lax.rem(blk + 1, n_blk), lax.rem(blk + n_blk - 1, n_blk)
    has_down, has_up = lat > 0, lat < n_lat - 1
    recv_y[...] = jnp.zeros_like(recv_y)
    barrier = pltpu.get_barrier_semaphore()
    for other in (up, down):
        pl.semaphore_signal(barrier, inc=1, device_id=(other, lat), device_id_type=MESH)

    @pl.when(has_down)
    def _():
        pl.semaphore_signal(barrier, inc=1, device_id=(blk, lat - 1), device_id_type=MESH)

    @pl.when(has_up)
    def _():
        pl.semaphore_signal(barrier, inc=1, device_id=(blk, lat + 1), device_id_type=MESH)

    shear_w[...] = jnp.zeros_like(shear_w)
    lame_w[...] = jnp.zeros_like(lame_w)
    for j in range(25):
        shear_w[8 * j : 8 * j + 5, :] = shear[5 * j : 5 * j + 5, :]
        lame_w[8 * j : 8 * j + 5, :] = lame[5 * j : 5 * j + 5, :]
    shear_w[...] = shear_w[...] * weight[...]
    lame_w[...] = lame_w[...] * weight[...]
    for c in range(COMPS):
        u[:, c * LANES : (c + 1) * LANES] = local_sum(gathered[c])
        v[:, c * LANES : (c + 1) * LANES] = local_sum(gathered[COMPS + c])
    mass = local_sum(gathered[2 * COMPS])
    inverse[...] = 1.0 / jnp.where(mass > 0.0, mass, 1.0)

    def forces(i, carry):
        force[i] = local_sum(gathered[FORCE_AT + i])
        return carry

    lax.fori_loop(0, STEPS * COMPS, forces, 0)

    pl.semaphore_wait(barrier, 2 + jnp.minimum(lat, 1) + jnp.minimum(n_lat - 1 - lat, 1))

    ex40, _, _ = lane_parts((40, LANES))
    _, ey8, _ = lane_parts((8, LANES))

    def cols(c):
        return slice(c * LANES, (c + 1) * LANES)

    def step(k, carry):
        high, low = parts(u[...])
        grads[...] = product(fwd_high[...], fwd_low[...], high, low)
        for s in range(2):
            g = [
                [grads[d * ROWS : (d + 1) * ROWS, cols(3 * s + q)] for q in range(3)]
                for d in range(3)
            ]
            trace = g[0][0] + g[1][1] + g[2][2]
            pressure = lame_w[...] * trace
            for d in range(3):
                for q in range(d, 3):
                    stress = shear_w[...] * (g[d][q] + g[q][d])
                    if d == q:
                        stress = stress + pressure
                    sh, sl = parts(stress)
                    flux_high[d * ROWS : (d + 1) * ROWS, cols(3 * s + q)] = sh
                    flux_low[d * ROWS : (d + 1) * ROWS, cols(3 * s + q)] = sl
                    if d != q:
                        flux_high[q * ROWS : (q + 1) * ROWS, cols(3 * s + d)] = sh
                        flux_low[q * ROWS : (q + 1) * ROWS, cols(3 * s + d)] = sl
            t = [[grads[d * ROWS + 5 : d * ROWS + 6, cols(3 * s + q)] for q in range(3)] for d in range(3)]
            third = (t[0][0] + t[1][1] + t[2][2]) / 3.0
            pieces = (
                t[0][0] - third,
                t[1][1] - third,
                0.5 * (t[0][1] + t[1][0]),
                0.5 * (t[0][2] + t[2][0]),
                0.5 * (t[1][2] + t[2][1]),
            )
            integrals[k, s] = jnp.concatenate(pieces + (jnp.zeros((3, LANES), jnp.float32),), axis=0)
        balance[...] = product(bwd_high[...], bwd_low[...], flux_high[...], flux_low[...])
        for c in range(COMPS):
            balance[:, cols(c)] = force[COMPS * k + c] - local_sum(balance[:, cols(c)])

        for q in range(3):
            low0, low1 = balance[0:40, cols(q)], balance[0:40, cols(3 + q)]
            top0, top1 = balance[160:200, cols(q)], balance[160:200, cols(3 + q)]
            send_x[0, :, cols(q)] = jnp.where(ex40 == 0, low0, pltpu.roll(low1, HALF_X, 1))
            send_x[1, :, cols(q)] = jnp.where(ex40 == 1, top0, pltpu.roll(top1, HALF_X, 1))
        copies = [
            pltpu.make_async_remote_copy(
                src_ref=send_x.at[side], dst_ref=recv_x.at[k, side],
                send_sem=sx.at[k, side], recv_sem=rx.at[k, side],
                device_id=(other, lat), device_id_type=MESH,
            )
            for side, other in ((0, down), (1, up))
        ]
        for copy in copies:
            copy.start()
        for copy in copies:
            copy.wait()
        for q in range(3):
            from_up, from_down = recv_x[k, 0, :, cols(q)], recv_x[k, 1, :, cols(q)]
            for s in range(2):
                c = 3 * s + q
                fd = pltpu.roll(from_down, HALF_X, 1) if s == 0 else from_down
                fu = pltpu.roll(from_up, HALF_X, 1) if s == 0 else from_up
                balance[0:40, cols(c)] = balance[0:40, cols(c)] + jnp.where(ex40 == 0, fd, 0.0)
                balance[160:200, cols(c)] = balance[160:200, cols(c)] + jnp.where(ex40 == 1, fu, 0.0)

        for a in range(5):
            for group in range(2):
                low_pack = jnp.zeros((8, LANES), jnp.float32)
                top_pack = jnp.zeros((8, LANES), jnp.float32)
                for slot in range(min(4, COMPS - 4 * group)):
                    c = 4 * group + slot
                    low_face = balance[40 * a : 40 * a + 8, cols(c)]
                    top_face = balance[40 * a + 32 : 40 * a + 40, cols(c)]
                    if slot:
                        low_face = pltpu.roll(low_face, slot * EZ, 1)
                    if slot < 3:
                        top_face = pltpu.roll(top_face, LANES - (3 - slot) * EZ, 1)
                    low_pack = jnp.where(ey8 == slot, low_face, low_pack)
                    top_pack = jnp.where(ey8 == slot, top_face, top_pack)
                send_y[0, 8 * a : 8 * a + 8, cols(group)] = low_pack
                send_y[1, 8 * a : 8 * a + 8, cols(group)] = top_pack

        to_down = pltpu.make_async_remote_copy(
            src_ref=send_y.at[0], dst_ref=recv_y.at[k, 0],
            send_sem=sy.at[k, 0], recv_sem=ry.at[k, 0],
            device_id=(blk, jnp.maximum(lat - 1, 0)), device_id_type=MESH,
        )
        to_up = pltpu.make_async_remote_copy(
            src_ref=send_y.at[1], dst_ref=recv_y.at[k, 1],
            send_sem=sy.at[k, 1], recv_sem=ry.at[k, 1],
            device_id=(blk, jnp.minimum(lat + 1, n_lat - 1)), device_id_type=MESH,
        )

        @pl.when(has_down)
        def _():
            to_down.start()

        @pl.when(has_up)
        def _():
            to_up.start()

        @pl.when(has_down)
        def _():
            to_down.wait_send()
            to_up.wait_recv()

        @pl.when(has_up)
        def _():
            to_up.wait_send()
            to_down.wait_recv()

        for a in range(5):
            for c in range(COMPS):
                group, slot = c // 4, c % 4
                fd = recv_y[k, 1, 8 * a : 8 * a + 8, cols(group)]
                fu = recv_y[k, 0, 8 * a : 8 * a + 8, cols(group)]
                if slot:
                    fd = pltpu.roll(fd, LANES - slot * EZ, 1)
                if slot < 3:
                    fu = pltpu.roll(fu, (3 - slot) * EZ, 1)
                r = 40 * a
                balance[r : r + 8, cols(c)] = balance[r : r + 8, cols(c)] + jnp.where(ey8 == 0, fd, 0.0)
                balance[r + 32 : r + 40, cols(c)] = balance[r + 32 : r + 40, cols(c)] + jnp.where(
                    ey8 == EYL - 1, fu, 0.0
                )
        for c in range(COMPS):
            speed = v[:, cols(c)] + balance[:, cols(c)] * inverse[...]
            v[:, cols(c)] = speed
            u[:, cols(c)] = u[:, cols(c)] + speed
        return carry

    lax.fori_loop(0, STEPS, step, 0)
    for c in range(COMPS):
        state[c * ROWS : (c + 1) * ROWS, :] = u[:, cols(c)]
        state[(COMPS + c) * ROWS : (COMPS + c + 1) * ROWS, :] = v[:, cols(c)]
    state[2 * COMPS * ROWS :, :] = jnp.zeros((4 * ROWS, LANES), jnp.float32)


def scatter_kernel(numbers, spectra, state, integrals, out_u, out_v, spectrum, table, stage):
    def point(p, row, own, last):
        block = state[pl.ds(row, 16, stride=ROWS), :]
        full = jnp.concatenate([block, jnp.zeros((LANES - 16, LANES), jnp.float32)], axis=0)
        stage[...] = full.T
        for e in own:
            table[pl.ds(numbers[p, e], 1), :] = stage[pl.ds(e, 1), :]

    over_points(point)
    count = out_u.shape[2]

    def emit(at, width):
        block = table[pl.ds(at, LANES), :].T
        for s in range(2):
            out_u[s, :, pl.ds(at, width)] = block[3 * s : 3 * s + 3, :width]
            out_v[s, :, pl.ds(at, width)] = block[COMPS + 3 * s : COMPS + 3 * s + 3, :width]

    def turn(i, carry):
        emit(pl.multiple_of(i * LANES, LANES), LANES)
        return carry

    lax.fori_loop(0, count // LANES, turn, 0)
    if count % LANES:
        emit(count // LANES * LANES, count % LANES)

    def frequency(f, carry):
        for part in range(2):
            for s in range(2):
                total = spectra[part, STEPS * f] * integrals[0, s, 0:5, :]
                for k in range(1, STEPS):
                    total = total + spectra[part, STEPS * f + k] * integrals[k, s, 0:5, :]
                spectrum[part, f, s] = total
        return carry

    lax.fori_loop(0, NFREQ, frequency, 0)


def local(n_blk, n_lat, displacement, velocity, lumped_mass, shear, lame, sources, numbers, event_frequency):
    nodes = displacement.shape[2]
    padded = -(-nodes // LANES) * LANES
    omega = jnp.pi * (1.0 + jnp.arange(NFREQ, dtype=jnp.float32)) / (NFREQ + 1.0)
    onehot = (event_frequency[:, :, None] == jnp.arange(NFREQ, dtype=jnp.int32)[None, None, :])
    chosen = jnp.sum(onehot.astype(jnp.float32) * omega[None, None, :], axis=2)
    times = 1.0 + jnp.arange(STEPS, dtype=jnp.float32)
    pulse = jnp.cos(times[:, None, None] * chosen[None]).astype(jnp.bfloat16)
    phase = omega[:, None] * times[None, :]
    spectra = jnp.stack([jnp.cos(phase), -jnp.sin(phase)]).reshape(2, NFREQ * STEPS)
    force = jnp.einsum(
        "ce,eqn->cqn", pulse.reshape(STEPS * 2, -1), sources, preferred_element_type=jnp.float32
    )
    values = jnp.concatenate(
        [
            displacement.reshape(COMPS, nodes),
            velocity.reshape(COMPS, nodes),
            lumped_mass[None],
            jnp.zeros((3, nodes), jnp.float32),
            force.reshape(STEPS * COMPS, nodes),
        ],
        axis=0,
    )
    values = jnp.pad(values, ((0, 0), (0, padded - nodes)))
    in_smem = pl.BlockSpec(memory_space=pltpu.SMEM)
    in_vmem = pl.BlockSpec(memory_space=VMEM)
    gathered = pl.pallas_call(
        gather_kernel,
        out_shape=jax.ShapeDtypeStruct((TABLE * ROWS, LANES), jnp.float32),
        in_specs=[in_smem, in_vmem],
        out_specs=in_vmem,
        scratch_shapes=[VMEM((padded, LANES), jnp.float32), VMEM((LANES, LANES), jnp.float32)],
        compiler_params=pltpu.CompilerParams(vmem_limit_bytes=LIMIT),
        name="gather_nodes",
    )(numbers, values)
    forward, backward, weight = operators()
    wide = COMPS * LANES
    f32, bf16 = jnp.float32, jnp.bfloat16
    state, integrals = pl.pallas_call(
        functools.partial(step_kernel, n_blk, n_lat),
        out_shape=(
            jax.ShapeDtypeStruct((16 * ROWS, LANES), f32),
            jax.ShapeDtypeStruct((STEPS, 2, 8, LANES), f32),
        ),
        in_specs=[in_vmem] * 8,
        out_specs=(in_vmem, in_vmem),
        scratch_shapes=[
            VMEM((ROWS, wide), f32),
            VMEM((ROWS, wide), f32),
            VMEM((STEPS * COMPS, ROWS, LANES), f32),
            VMEM((ROWS, LANES), f32),
            VMEM((ROWS, LANES), f32),
            VMEM((ROWS, LANES), f32),
            VMEM((3 * ROWS, wide), f32),
            VMEM((3 * ROWS, wide), bf16),
            VMEM((3 * ROWS, wide), bf16),
            VMEM((ROWS, wide), f32),
            VMEM((2, 40, 3 * LANES), f32),
            VMEM((2, 40, 2 * LANES), f32),
            VMEM((STEPS, 2, 40, 3 * LANES), f32),
            VMEM((STEPS, 2, 40, 2 * LANES), f32),
            pltpu.SemaphoreType.DMA((STEPS, 2)),
            pltpu.SemaphoreType.DMA((STEPS, 2)),
            pltpu.SemaphoreType.DMA((STEPS, 2)),
            pltpu.SemaphoreType.DMA((STEPS, 2)),
        ],
        compiler_params=pltpu.CompilerParams(
            vmem_limit_bytes=LIMIT, collective_id=0, has_side_effects=True
        ),
        name="time_steps",
    )(
        gathered.reshape(TABLE, ROWS, LANES), shear, lame, jnp.asarray(weight),
        *two_parts(forward), *two_parts(backward),
    )
    return pl.pallas_call(
        scatter_kernel,
        out_shape=(
            jax.ShapeDtypeStruct(displacement.shape, f32),
            jax.ShapeDtypeStruct(displacement.shape, f32),
            jax.ShapeDtypeStruct((2, NFREQ, 2, 5, LANES), f32),
        ),
        in_specs=[in_smem, in_smem, in_vmem, in_vmem],
        out_specs=(in_vmem,) * 3,
        scratch_shapes=[VMEM((padded, LANES), f32), VMEM((LANES, LANES), f32)],
        compiler_params=pltpu.CompilerParams(vmem_limit_bytes=LIMIT),
        name="scatter_nodes",
    )(numbers, spectra, state, integrals)


def solution(mesh):
    both = ("blk", "lat")
    return jax.shard_map(
        functools.partial(local, mesh.shape["blk"], mesh.shape["lat"]),
        mesh=mesh,
        in_specs=(
            P(None, None, both), P(None, None, both), P(both), P(None, both), P(None, both),
            P(None, None, both), P(None, both), P(),
        ),
        out_specs=(P(None, None, both), P(None, None, both), P(None, None, None, None, both)),
        check_vma=False,
    )
```

```python
import functools
import math

import jax
import jax.numpy as jnp
import ml_dtypes
import numpy as np
from jax import lax
from jax.experimental import pallas as pl
from jax.experimental.pallas import tpu as pltpu
from jax.sharding import PartitionSpec as P

EXB = 2
EYL = 4
EZ = 16
NFREQ = 32
STEPS = 4
ELEMS = EXB * EYL * EZ
LANES = 128
ROWS = 208
COMPS = 6
TABLE = 40
FORCE_AT = 16
HALF_X = EYL * EZ
VMEM = pltpu.VMEM
MESH = pl.DeviceIdType.MESH
LIMIT = 56 * 1024 * 1024


def row_of(a, b, c):
    return (5 * a + b) * 8 + c


def gll():
    points = np.array([-1.0, -math.sqrt(3.0 / 7.0), 0.0, math.sqrt(3.0 / 7.0), 1.0])
    weights = np.array([0.1, 49.0 / 90.0, 32.0 / 45.0, 49.0 / 90.0, 0.1])
    products = np.ones(5)
    for i in range(5):
        for j in range(5):
            if i != j:
                products[i] *= points[i] - points[j]
    derivative = np.zeros((5, 5))
    for i in range(5):
        for j in range(5):
            if i != j:
                derivative[i, j] = products[i] / products[j] / (points[i] - points[j])
        derivative[i, i] = -np.sum(derivative[i])
    cube = weights[:, None, None] * weights[None, :, None] * weights[None, None, :] / 8.0
    return derivative, cube


def operators():
    derivative, cube = gll()
    forward = np.zeros((3, ROWS, ROWS))
    weight = np.zeros((ROWS, LANES))
    for a in range(5):
        for b in range(5):
            for c in range(5):
                r = row_of(a, b, c)
                weight[r] = cube[a, b, c]
                for l in range(5):
                    forward[0, r, row_of(l, b, c)] += 2.0 * derivative[a, l]
                    forward[1, r, row_of(a, l, c)] += 2.0 * derivative[b, l]
                    forward[2, r, row_of(a, b, l)] += 2.0 * derivative[c, l]
    backward = forward.transpose(2, 0, 1).reshape(ROWS, 3 * ROWS).copy()
    for d in range(3):
        forward[d, 5] = weight[:, 0] @ forward[d]
    return forward.reshape(3 * ROWS, ROWS), backward, weight.astype(np.float32)


def two_parts(values):
    high = values.astype(np.float32).astype(ml_dtypes.bfloat16)
    low = (values - high.astype(np.float64)).astype(ml_dtypes.bfloat16)
    return jnp.asarray(high), jnp.asarray(low)


def owner_classes():
    every = list(range(ELEMS))
    out = []
    for last_a in (False, True):
        for last_b in (False, True):
            for last_c in (False, True):
                own = [
                    e
                    for e in every
                    if (not last_a or e // HALF_X == EXB - 1)
                    and (not last_b or e // EZ % EYL == EYL - 1)
                    and (not last_c or e % EZ == EZ - 1)
                ]
                out.append((last_a, last_b, last_c, own))
    return out


def over_points(body):
    for last_a, last_b, last_c, own in owner_classes():
        na, nb, nc = (1 if last_a else 4), (1 if last_b else 4), (1 if last_c else 4)

        def step(i, carry, own=own, na=na, nb=nb, nc=nc, la=last_a, lb=last_b, lc=last_c):
            a = 4 if la else i // (nb * nc)
            b = 4 if lb else (i // nc) % nb
            c = 4 if lc else i % nc
            body(25 * a + 5 * b + c, (5 * a + b) * 8 + c, own, (la, lb, lc))
            return carry

        lax.fori_loop(0, na * nb * nc, step, 0)


def lane_parts(shape):
    lane = lax.broadcasted_iota(jnp.int32, shape, len(shape) - 1)
    return lane // HALF_X, lane // EZ % EYL, lane % EZ


def in_batches(items, size):
    return [items[i : i + size] for i in range(0, len(items), size)]


def gather_kernel(numbers, u, v, mass, force, out, table, stage):
    count = u.shape[2]
    stage[...] = jnp.zeros_like(stage)

    def collect(at, width):
        cols = pl.ds(at, width)
        for q in range(3):
            stage[2 * q : 2 * q + 2, :width] = u[q, :, cols]
            stage[COMPS + 2 * q : COMPS + 2 * q + 2, :width] = v[q, :, cols]
            rows = slice(FORCE_AT + 2 * STEPS * q, FORCE_AT + 2 * STEPS * (q + 1))
            stage[rows, :width] = force[q, :, cols]
        stage[2 * COMPS : 2 * COMPS + 1, :width] = mass[:, cols]
        table[pl.ds(at, LANES), :] = stage[...].T

    def turn(i, carry):
        collect(pl.multiple_of(i * LANES, LANES), LANES)
        return carry

    lax.fori_loop(0, count // LANES, turn, 0)
    if count % LANES:
        collect(count // LANES * LANES, count % LANES)
    out[...] = jnp.zeros_like(out)
    ex, ey, ez = lane_parts((TABLE, LANES))

    def point(p, row, own, last):
        for batch in in_batches(own, 32):
            found = [table[pl.ds(numbers[p, e], 1), :] for e in batch]
            for e, line in zip(batch, found):
                stage[pl.ds(e, 1), :] = line
        block = stage[...].T[:TABLE]
        keep = None
        for flag, part, top in zip(last, (ex, ey, ez), (EXB - 1, EYL - 1, EZ - 1)):
            if flag:
                keep = (part == top) if keep is None else keep & (part == top)
        if keep is not None:
            block = jnp.where(keep, block, 0.0)
        out[pl.ds(row, TABLE, stride=ROWS), :] = block

    over_points(point)


def local_sum(x):
    x = x.reshape(ROWS // 8, 8, LANES)
    sub = lax.broadcasted_iota(jnp.int32, x.shape, 1)
    ez = lax.broadcasted_iota(jnp.int32, x.shape, 2) % EZ
    turned = pltpu.roll(x, 4, 1)
    x = x + jnp.where((sub == 4) & (ez < EZ - 1), pltpu.roll(turned, LANES - 1, 2), 0.0)
    x = x + jnp.where((sub == 0) & (ez > 0), pltpu.roll(turned, 1, 2), 0.0)
    ex, ey, _ = lane_parts((8, LANES))
    blocks = [x[i] for i in range(ROWS // 8)]
    for a in range(5):
        low, high = blocks[5 * a], blocks[5 * a + 4]
        blocks[5 * a] = low + jnp.where(ey > 0, pltpu.roll(high, EZ, 1), 0.0)
        blocks[5 * a + 4] = high + jnp.where(ey < EYL - 1, pltpu.roll(low, LANES - EZ, 1), 0.0)
    for b in range(5):
        low, high = blocks[b], blocks[20 + b]
        blocks[b] = low + jnp.where(ex > 0, pltpu.roll(high, HALF_X, 1), 0.0)
        blocks[20 + b] = high + jnp.where(ex < EXB - 1, pltpu.roll(low, LANES - HALF_X, 1), 0.0)
    return jnp.concatenate(blocks, axis=0)


def parts(x):
    high = x.astype(jnp.bfloat16)
    return high, (x - high.astype(jnp.float32)).astype(jnp.bfloat16)


def product(left_high, left_low, high, low):
    dot = functools.partial(jnp.dot, preferred_element_type=jnp.float32)
    return dot(left_high, high) + dot(left_high, low) + dot(left_low, high)


def step_kernel(
    n_blk, n_lat,
    gathered, shear, lame, weight, fwd_high, fwd_low, bwd_high, bwd_low,
    state, integrals,
    u, v, force, inverse, shear_w, lame_w, grads, flux_high, flux_low, balance,
    send_x, send_y, send_c, recv_x, recv_y, recv_c, sx, rx, sy, ry, sc, rc,
):
    blk, lat = lax.axis_index("blk"), lax.axis_index("lat")
    up, down = lax.rem(blk + 1, n_blk), lax.rem(blk + n_blk - 1, n_blk)
    has_down, has_up = lat > 0, lat < n_lat - 1
    recv_y[...] = jnp.zeros_like(recv_y)
    recv_c[...] = jnp.zeros_like(recv_c)
    barrier = pltpu.get_barrier_semaphore()
    for other in (up, down):
        pl.semaphore_signal(barrier, inc=1, device_id=(other, lat), device_id_type=MESH)

    @pl.when(has_down)
    def _():
        for other in (blk, up, down):
            pl.semaphore_signal(barrier, inc=1, device_id=(other, lat - 1), device_id_type=MESH)

    @pl.when(has_up)
    def _():
        for other in (blk, up, down):
            pl.semaphore_signal(barrier, inc=1, device_id=(other, lat + 1), device_id_type=MESH)

    shear_w[...] = jnp.zeros_like(shear_w)
    lame_w[...] = jnp.zeros_like(lame_w)
    for j in range(25):
        shear_w[8 * j : 8 * j + 5, :] = shear[5 * j : 5 * j + 5, :]
        lame_w[8 * j : 8 * j + 5, :] = lame[5 * j : 5 * j + 5, :]
    shear_w[...] = shear_w[...] * weight[...]
    lame_w[...] = lame_w[...] * weight[...]
    for c in range(COMPS):
        at = 2 * (c % 3) + c // 3
        u[:, c * LANES : (c + 1) * LANES] = local_sum(gathered[at])
        v[:, c * LANES : (c + 1) * LANES] = local_sum(gathered[COMPS + at])
    mass = local_sum(gathered[2 * COMPS])
    inverse[...] = 1.0 / jnp.where(mass > 0.0, mass, 1.0)

    def forces(i, carry):
        k, c = i // COMPS, i % COMPS
        force[i] = local_sum(gathered[FORCE_AT + 2 * STEPS * (c % 3) + 2 * k + c // 3])
        return carry

    lax.fori_loop(0, STEPS * COMPS, forces, 0)

    pl.semaphore_wait(barrier, 2 + 3 * jnp.minimum(lat, 1) + 3 * jnp.minimum(n_lat - 1 - lat, 1))

    ex40, _, _ = lane_parts((40, LANES))
    _, ey8, _ = lane_parts((8, LANES))
    slot8 = lax.broadcasted_iota(jnp.int32, (8, LANES), 1) // EZ
    corner_places = ((0, 0), (32, EYL - 1), (160, EYL * (EXB - 1)), (192, EYL * EXB - 1))

    def cols(c):
        return slice(c * LANES, (c + 1) * LANES)

    def step(k, carry):
        high, low = parts(u[...])
        grads[...] = product(fwd_high[...], fwd_low[...], high, low)
        for s in range(2):
            g = [
                [grads[d * ROWS : (d + 1) * ROWS, cols(3 * s + q)] for q in range(3)]
                for d in range(3)
            ]
            trace = g[0][0] + g[1][1] + g[2][2]
            pressure = lame_w[...] * trace
            for d in range(3):
                for q in range(d, 3):
                    stress = shear_w[...] * (g[d][q] + g[q][d])
                    if d == q:
                        stress = stress + pressure
                    sh, sl = parts(stress)
                    flux_high[d * ROWS : (d + 1) * ROWS, cols(3 * s + q)] = sh
                    flux_low[d * ROWS : (d + 1) * ROWS, cols(3 * s + q)] = sl
                    if d != q:
                        flux_high[q * ROWS : (q + 1) * ROWS, cols(3 * s + d)] = sh
                        flux_low[q * ROWS : (q + 1) * ROWS, cols(3 * s + d)] = sl
            t = [[grads[d * ROWS + 5 : d * ROWS + 6, cols(3 * s + q)] for q in range(3)] for d in range(3)]
            third = (t[0][0] + t[1][1] + t[2][2]) / 3.0
            pieces = (
                t[0][0] - third,
                t[1][1] - third,
                0.5 * (t[0][1] + t[1][0]),
                0.5 * (t[0][2] + t[2][0]),
                0.5 * (t[1][2] + t[2][1]),
            )
            for m in range(5):
                integrals[k, m, s : s + 1, :] = pieces[m]
        balance[...] = product(bwd_high[...], bwd_low[...], flux_high[...], flux_low[...])
        for c in range(COMPS):
            balance[:, cols(c)] = force[COMPS * k + c] - local_sum(balance[:, cols(c)])

        for q in range(3):
            low0, low1 = balance[0:40, cols(q)], balance[0:40, cols(3 + q)]
            top0, top1 = balance[160:200, cols(q)], balance[160:200, cols(3 + q)]
            send_x[0, :, cols(q)] = jnp.where(ex40 == 0, low0, pltpu.roll(low1, HALF_X, 1))
            send_x[1, :, cols(q)] = jnp.where(ex40 == 1, top0, pltpu.roll(top1, HALF_X, 1))
        for a in range(5):
            for group in range(2):
                low_pack = jnp.zeros((8, LANES), jnp.float32)
                top_pack = jnp.zeros((8, LANES), jnp.float32)
                for slot in range(min(4, COMPS - 4 * group)):
                    c = 4 * group + slot
                    low_face = balance[40 * a : 40 * a + 8, cols(c)]
                    top_face = balance[40 * a + 32 : 40 * a + 40, cols(c)]
                    if slot:
                        low_face = pltpu.roll(low_face, slot * EZ, 1)
                    if slot < 3:
                        top_face = pltpu.roll(top_face, LANES - (3 - slot) * EZ, 1)
                    low_pack = jnp.where(ey8 == slot, low_face, low_pack)
                    top_pack = jnp.where(ey8 == slot, top_face, top_pack)
                send_y[0, 8 * a : 8 * a + 8, cols(group)] = low_pack
                send_y[1, 8 * a : 8 * a + 8, cols(group)] = top_pack

        for corner in range(4):
            r, home = corner_places[corner]
            pack = jnp.zeros((8, LANES), jnp.float32)
            for c in range(COMPS):
                edge = balance[r : r + 8, cols(c)]
                shift = (c - home) * EZ % LANES
                if shift:
                    edge = pltpu.roll(edge, shift, 1)
                pack = jnp.where(slot8 == c, edge, pack)
            send_c[corner] = pack

        def copy(src, dst, ss, rs, other, row):
            return pltpu.make_async_remote_copy(
                src_ref=src, dst_ref=dst, send_sem=ss, recv_sem=rs,
                device_id=(other, row), device_id_type=MESH,
            )

        rows = (jnp.maximum(lat - 1, 0), jnp.minimum(lat + 1, n_lat - 1))
        x_copies = [
            copy(send_x.at[i], recv_x.at[k, i], sx.at[k, i], rx.at[k, i], (down, up)[i], lat)
            for i in range(2)
        ]
        y_copies = [
            copy(send_y.at[i], recv_y.at[k, i], sy.at[k, i], ry.at[k, i], blk, rows[i])
            for i in range(2)
        ]
        c_copies = [
            copy(send_c.at[i], recv_c.at[k, i], sc.at[k, i], rc.at[k, i], (down, up)[i // 2], rows[i % 2])
            for i in range(4)
        ]
        to_down = [y_copies[0], c_copies[0], c_copies[2]]
        to_up = [y_copies[1], c_copies[1], c_copies[3]]
        for one in x_copies:
            one.start()

        @pl.when(has_down)
        def _():
            for one in to_down:
                one.start()

        @pl.when(has_up)
        def _():
            for one in to_up:
                one.start()

        for c in range(COMPS):
            speed = v[:, cols(c)] + balance[:, cols(c)] * inverse[...]
            v[:, cols(c)] = speed
            u[:, cols(c)] = u[:, cols(c)] + speed

        for one in x_copies:
            one.wait()

        @pl.when(has_down)
        def _():
            for one in to_down:
                one.wait_send()
            for one in to_up:
                one.wait_recv()

        @pl.when(has_up)
        def _():
            for one in to_up:
                one.wait_send()
            for one in to_down:
                one.wait_recv()

        def bump(r, size, c, extra):
            extra = extra * inverse[r : r + size, :]
            v[r : r + size, cols(c)] = v[r : r + size, cols(c)] + extra
            u[r : r + size, cols(c)] = u[r : r + size, cols(c)] + extra

        for q in range(3):
            from_up, from_down = recv_x[k, 0, :, cols(q)], recv_x[k, 1, :, cols(q)]
            for s in range(2):
                fd = pltpu.roll(from_down, HALF_X, 1) if s == 0 else from_down
                fu = pltpu.roll(from_up, HALF_X, 1) if s == 0 else from_up
                bump(0, 40, 3 * s + q, jnp.where(ex40 == 0, fd, 0.0))
                bump(160, 40, 3 * s + q, jnp.where(ex40 == 1, fu, 0.0))
        for a in range(5):
            for c in range(COMPS):
                group, slot = c // 4, c % 4
                fd = recv_y[k, 1, 8 * a : 8 * a + 8, cols(group)]
                fu = recv_y[k, 0, 8 * a : 8 * a + 8, cols(group)]
                if slot:
                    fd = pltpu.roll(fd, LANES - slot * EZ, 1)
                if slot < 3:
                    fu = pltpu.roll(fu, (3 - slot) * EZ, 1)
                bump(40 * a, 8, c, jnp.where(ey8 == 0, fd, 0.0))
                bump(40 * a + 32, 8, c, jnp.where(ey8 == EYL - 1, fu, 0.0))
        for corner in range(4):
            r, home = corner_places[corner]
            pack = recv_c[k, 3 - corner]
            for c in range(COMPS):
                shift = (home - c) * EZ % LANES
                edge = pltpu.roll(pack, shift, 1) if shift else pack
                bump(r, 8, c, jnp.where(slot8 == home, edge, 0.0))
        return carry

    lax.fori_loop(0, STEPS, step, 0)
    for c in range(COMPS):
        at = 2 * (c % 3) + c // 3
        state[at * ROWS : (at + 1) * ROWS, :] = u[:, cols(c)]
        state[(COMPS + at) * ROWS : (COMPS + at + 1) * ROWS, :] = v[:, cols(c)]
    state[2 * COMPS * ROWS :, :] = jnp.zeros((4 * ROWS, LANES), jnp.float32)


def scatter_kernel(numbers, spectra, state, integrals, out_u, out_v, spectrum, table, stage):
    def point(p, row, own, last):
        block = state[pl.ds(row, 16, stride=ROWS), :]
        full = jnp.concatenate([block, jnp.zeros((LANES - 16, LANES), jnp.float32)], axis=0)
        stage[...] = full.T
        for batch in in_batches(own, 32):
            lines = [stage[pl.ds(e, 1), :] for e in batch]
            for e, line in zip(batch, lines):
                table[pl.ds(numbers[p, e], 1), :] = line

    over_points(point)
    count = out_u.shape[2]

    def emit(at, width):
        block = table[pl.ds(at, LANES), :].T
        for q in range(3):
            out_u[q, :, pl.ds(at, width)] = block[2 * q : 2 * q + 2, :width]
            out_v[q, :, pl.ds(at, width)] = block[COMPS + 2 * q : COMPS + 2 * q + 2, :width]

    def turn(i, carry):
        emit(pl.multiple_of(i * LANES, LANES), LANES)
        return carry

    lax.fori_loop(0, count // LANES, turn, 0)
    if count % LANES:
        emit(count // LANES * LANES, count % LANES)

    def frequency(f, carry):
        for part in range(2):
            total = spectra[part, STEPS * f] * integrals[0]
            for k in range(1, STEPS):
                total = total + spectra[part, STEPS * f + k] * integrals[k]
            spectrum[part, f] = total
        return carry

    lax.fori_loop(0, NFREQ, frequency, 0)


def local(n_blk, n_lat, displacement, velocity, lumped_mass, shear, lame, sources, numbers, event_frequency):
    nodes = displacement.shape[2]
    padded = -(-nodes // LANES) * LANES
    omega = jnp.pi * (1.0 + jnp.arange(NFREQ, dtype=jnp.float32)) / (NFREQ + 1.0)
    onehot = (event_frequency[:, :, None] == jnp.arange(NFREQ, dtype=jnp.int32)[None, None, :])
    chosen = jnp.sum(onehot.astype(jnp.float32) * omega[None, None, :], axis=2)
    times = 1.0 + jnp.arange(STEPS, dtype=jnp.float32)
    pulse = jnp.cos(times[:, None, None] * chosen[None]).astype(jnp.bfloat16)
    phase = omega[:, None] * times[None, :]
    spectra = jnp.stack([jnp.cos(phase), -jnp.sin(phase)]).reshape(2, NFREQ * STEPS)
    force = jnp.einsum(
        "ce,eqn->qcn", pulse.reshape(STEPS * 2, -1), sources, preferred_element_type=jnp.float32
    )
    in_smem = pl.BlockSpec(memory_space=pltpu.SMEM)
    in_vmem = pl.BlockSpec(memory_space=VMEM)
    gathered = pl.pallas_call(
        gather_kernel,
        out_shape=jax.ShapeDtypeStruct((TABLE * ROWS, LANES), jnp.float32),
        in_specs=[in_smem] + [in_vmem] * 4,
        out_specs=in_vmem,
        scratch_shapes=[VMEM((padded, LANES), jnp.float32), VMEM((LANES, LANES), jnp.float32)],
        compiler_params=pltpu.CompilerParams(vmem_limit_bytes=LIMIT),
        name="gather_nodes",
    )(
        numbers, displacement.transpose(1, 0, 2), velocity.transpose(1, 0, 2), lumped_mass[None], force
    )
    forward, backward, weight = operators()
    wide = COMPS * LANES
    f32, bf16 = jnp.float32, jnp.bfloat16
    state, integrals = pl.pallas_call(
        functools.partial(step_kernel, n_blk, n_lat),
        out_shape=(
            jax.ShapeDtypeStruct((16 * ROWS, LANES), f32),
            jax.ShapeDtypeStruct((STEPS, 5, 2, LANES), f32),
        ),
        in_specs=[in_vmem] * 8,
        out_specs=(in_vmem, in_vmem),
        scratch_shapes=[
            VMEM((ROWS, wide), f32),
            VMEM((ROWS, wide), f32),
            VMEM((STEPS * COMPS, ROWS, LANES), f32),
            VMEM((ROWS, LANES), f32),
            VMEM((ROWS, LANES), f32),
            VMEM((ROWS, LANES), f32),
            VMEM((3 * ROWS, wide), f32),
            VMEM((3 * ROWS, wide), bf16),
            VMEM((3 * ROWS, wide), bf16),
            VMEM((ROWS, wide), f32),
            VMEM((2, 40, 3 * LANES), f32),
            VMEM((2, 40, 2 * LANES), f32),
            VMEM((4, 8, LANES), f32),
            VMEM((STEPS, 2, 40, 3 * LANES), f32),
            VMEM((STEPS, 2, 40, 2 * LANES), f32),
            VMEM((STEPS, 4, 8, LANES), f32),
            pltpu.SemaphoreType.DMA((STEPS, 2)),
            pltpu.SemaphoreType.DMA((STEPS, 2)),
            pltpu.SemaphoreType.DMA((STEPS, 2)),
            pltpu.SemaphoreType.DMA((STEPS, 2)),
            pltpu.SemaphoreType.DMA((STEPS, 4)),
            pltpu.SemaphoreType.DMA((STEPS, 4)),
        ],
        compiler_params=pltpu.CompilerParams(
            vmem_limit_bytes=LIMIT, collective_id=0, has_side_effects=True
        ),
        name="time_steps",
    )(
        gathered.reshape(TABLE, ROWS, LANES), shear, lame, jnp.asarray(weight),
        *two_parts(forward), *two_parts(backward),
    )
    final_u, final_v, spectrum = pl.pallas_call(
        scatter_kernel,
        out_shape=(
            jax.ShapeDtypeStruct((3, 2, nodes), f32),
            jax.ShapeDtypeStruct((3, 2, nodes), f32),
            jax.ShapeDtypeStruct((2, NFREQ, 5, 2, LANES), f32),
        ),
        in_specs=[in_smem, in_smem, in_vmem, in_vmem],
        out_specs=(in_vmem,) * 3,
        scratch_shapes=[VMEM((padded, LANES), f32), VMEM((LANES, LANES), f32)],
        compiler_params=pltpu.CompilerParams(vmem_limit_bytes=LIMIT),
        name="scatter_nodes",
    )(numbers, spectra, state, integrals)
    return (
        final_u.transpose(1, 0, 2),
        final_v.transpose(1, 0, 2),
        spectrum.transpose(0, 1, 3, 2, 4),
    )


def solution(mesh):
    both = ("blk", "lat")
    return jax.shard_map(
        functools.partial(local, mesh.shape["blk"], mesh.shape["lat"]),
        mesh=mesh,
        in_specs=(
            P(None, None, both), P(None, None, both), P(both), P(None, both), P(None, both),
            P(None, None, both), P(None, both), P(),
        ),
        out_specs=(P(None, None, both), P(None, None, both), P(None, None, None, None, both)),
        check_vma=False,
    )
```

```python
import functools
import math

import jax
import jax.numpy as jnp
import ml_dtypes
import numpy as np
from jax import lax
from jax.experimental import pallas as pl
from jax.experimental.pallas import tpu as pltpu
from jax.sharding import PartitionSpec as P

EXB = 2
EYL = 4
EZ = 16
NFREQ = 32
STEPS = 4
ELEMS = EXB * EYL * EZ
LANES = 128
ROWS = 208
COMPS = 6
TABLE = 40
FORCE_AT = 16
HALF_X = EYL * EZ
VMEM = pltpu.VMEM
MESH = pl.DeviceIdType.MESH
LIMIT = 56 * 1024 * 1024


def row_of(a, b, c):
    return (5 * a + b) * 8 + c


def gll():
    points = np.array([-1.0, -math.sqrt(3.0 / 7.0), 0.0, math.sqrt(3.0 / 7.0), 1.0])
    weights = np.array([0.1, 49.0 / 90.0, 32.0 / 45.0, 49.0 / 90.0, 0.1])
    products = np.ones(5)
    for i in range(5):
        for j in range(5):
            if i != j:
                products[i] *= points[i] - points[j]
    derivative = np.zeros((5, 5))
    for i in range(5):
        for j in range(5):
            if i != j:
                derivative[i, j] = products[i] / products[j] / (points[i] - points[j])
        derivative[i, i] = -np.sum(derivative[i])
    cube = weights[:, None, None] * weights[None, :, None] * weights[None, None, :] / 8.0
    return derivative, cube


def operators():
    derivative, cube = gll()
    forward = np.zeros((3, ROWS, ROWS))
    weight = np.zeros((ROWS, LANES))
    for a in range(5):
        for b in range(5):
            for c in range(5):
                r = row_of(a, b, c)
                weight[r] = cube[a, b, c]
                for l in range(5):
                    forward[0, r, row_of(l, b, c)] += 2.0 * derivative[a, l]
                    forward[1, r, row_of(a, l, c)] += 2.0 * derivative[b, l]
                    forward[2, r, row_of(a, b, l)] += 2.0 * derivative[c, l]
    backward = forward.transpose(2, 0, 1).reshape(ROWS, 3 * ROWS).copy()
    for d in range(3):
        forward[d, 5] = weight[:, 0] @ forward[d]
    return forward.reshape(3 * ROWS, ROWS), backward, weight.astype(np.float32)


def two_parts(values):
    high = values.astype(np.float32).astype(ml_dtypes.bfloat16)
    low = (values - high.astype(np.float64)).astype(ml_dtypes.bfloat16)
    return jnp.asarray(high), jnp.asarray(low)


def owner_classes():
    every = list(range(ELEMS))
    out = []
    for last_a in (False, True):
        for last_b in (False, True):
            for last_c in (False, True):
                own = [
                    e
                    for e in every
                    if (not last_a or e // HALF_X == EXB - 1)
                    and (not last_b or e // EZ % EYL == EYL - 1)
                    and (not last_c or e % EZ == EZ - 1)
                ]
                out.append((last_a, last_b, last_c, own))
    return out


def over_points(body):
    for last_a, last_b, last_c, own in owner_classes():
        na, nb, nc = (1 if last_a else 4), (1 if last_b else 4), (1 if last_c else 4)
        moves = [
            (x, y, z)
            for x in range(EXB if last_a else 1)
            for y in range(EYL if last_b else 1)
            for z in range(EZ if last_c else 1)
        ]
        moves = moves[: na * nb * nc]

        def step(group, carry, own=own, nb=nb, nc=nc, la=last_a, lb=last_b, lc=last_c, moves=moves):
            members = []
            for j, move in enumerate(moves):
                i = group * len(moves) + j
                a = 4 if la else i // (nb * nc)
                b = 4 if lb else (i // nc) % nb
                c = 4 if lc else i % nc
                members.append((25 * a + 5 * b + c, (5 * a + b) * 8 + c, move))
            body(members, own, (la, lb, lc))
            return carry

        lax.fori_loop(0, na * nb * nc // len(moves), step, 0)


def shift_of(move):
    return move[0] * HALF_X + move[1] * EZ + move[2]


def chosen_lanes(flags, move, parts_of):
    keep = None
    for flag, part, top, back in zip(flags, parts_of, (EXB - 1, EYL - 1, EZ - 1), move):
        if flag:
            keep = (part == top - back) if keep is None else keep & (part == top - back)
    return keep


def lane_parts(shape):
    lane = lax.broadcasted_iota(jnp.int32, shape, len(shape) - 1)
    return lane // HALF_X, lane // EZ % EYL, lane % EZ


def in_batches(items, size):
    return [items[i : i + size] for i in range(0, len(items), size)]


def gather_kernel(numbers, u, v, mass, force, out, table, stage):
    count = u.shape[2]
    stage[...] = jnp.zeros_like(stage)

    def collect(at, width):
        cols = pl.ds(at, width)
        for q in range(3):
            stage[2 * q : 2 * q + 2, :width] = u[q, :, cols]
            stage[COMPS + 2 * q : COMPS + 2 * q + 2, :width] = v[q, :, cols]
            rows = slice(FORCE_AT + 2 * STEPS * q, FORCE_AT + 2 * STEPS * (q + 1))
            stage[rows, :width] = force[q, :, cols]
        stage[2 * COMPS : 2 * COMPS + 1, :width] = mass[:, cols]
        table[pl.ds(at, LANES), :TABLE] = stage[:TABLE, :].T

    def turn(i, carry):
        collect(pl.multiple_of(i * LANES, LANES), LANES)
        return carry

    lax.fori_loop(0, count // LANES, turn, 0)
    if count % LANES:
        collect(count // LANES * LANES, count % LANES)
    out[...] = jnp.zeros_like(out)
    ex, ey, ez = lane_parts((TABLE, LANES))

    def point(members, own, last):
        for p, row, move in members:
            for batch in in_batches(own, 16):
                found = [table[pl.ds(numbers[p, e], 1), :] for e in batch]
                for e, line in zip(batch, found):
                    stage[pl.ds(e - shift_of(move), 1), :] = line
        block = stage[:, :TABLE].T
        for p, row, move in members:
            moved = pltpu.roll(block, shift_of(move), 1) if shift_of(move) else block
            keep = chosen_lanes(last, (0, 0, 0), (ex, ey, ez))
            if keep is not None:
                moved = jnp.where(keep, moved, 0.0)
            out[pl.ds(row, TABLE, stride=ROWS), :] = moved

    over_points(point)


def local_sum(x):
    x = x.reshape(ROWS // 8, 8, LANES)
    sub = lax.broadcasted_iota(jnp.int32, x.shape, 1)
    ez = lax.broadcasted_iota(jnp.int32, x.shape, 2) % EZ
    turned = pltpu.roll(x, 4, 1)
    x = x + jnp.where((sub == 4) & (ez < EZ - 1), pltpu.roll(turned, LANES - 1, 2), 0.0)
    x = x + jnp.where((sub == 0) & (ez > 0), pltpu.roll(turned, 1, 2), 0.0)
    ex, ey, _ = lane_parts((8, LANES))
    blocks = [x[i] for i in range(ROWS // 8)]
    for a in range(5):
        low, high = blocks[5 * a], blocks[5 * a + 4]
        blocks[5 * a] = low + jnp.where(ey > 0, pltpu.roll(high, EZ, 1), 0.0)
        blocks[5 * a + 4] = high + jnp.where(ey < EYL - 1, pltpu.roll(low, LANES - EZ, 1), 0.0)
    for b in range(5):
        low, high = blocks[b], blocks[20 + b]
        blocks[b] = low + jnp.where(ex > 0, pltpu.roll(high, HALF_X, 1), 0.0)
        blocks[20 + b] = high + jnp.where(ex < EXB - 1, pltpu.roll(low, LANES - HALF_X, 1), 0.0)
    return jnp.concatenate(blocks, axis=0)


def parts(x):
    high = x.astype(jnp.bfloat16)
    return high, (x - high.astype(jnp.float32)).astype(jnp.bfloat16)


def product(left_high, left_low, high, low):
    dot = functools.partial(jnp.dot, preferred_element_type=jnp.float32)
    return dot(left_high, high) + dot(left_high, low) + dot(left_low, high)


def step_kernel(
    n_blk, n_lat,
    gathered, shear, lame, weight, fwd_high, fwd_low, bwd_high, bwd_low,
    state, integrals,
    u, v, force, inverse, shear_w, lame_w, grads, flux_high, flux_low, balance,
    send_x, send_y, send_c, recv_x, recv_y, recv_c, sx, rx, sy, ry, sc, rc,
):
    blk, lat = lax.axis_index("blk"), lax.axis_index("lat")
    up, down = lax.rem(blk + 1, n_blk), lax.rem(blk + n_blk - 1, n_blk)
    has_down, has_up = lat > 0, lat < n_lat - 1
    recv_y[...] = jnp.zeros_like(recv_y)
    recv_c[...] = jnp.zeros_like(recv_c)
    barrier = pltpu.get_barrier_semaphore()
    for other in (up, down):
        pl.semaphore_signal(barrier, inc=1, device_id=(other, lat), device_id_type=MESH)

    @pl.when(has_down)
    def _():
        for other in (blk, up, down):
            pl.semaphore_signal(barrier, inc=1, device_id=(other, lat - 1), device_id_type=MESH)

    @pl.when(has_up)
    def _():
        for other in (blk, up, down):
            pl.semaphore_signal(barrier, inc=1, device_id=(other, lat + 1), device_id_type=MESH)

    shear_w[...] = jnp.zeros_like(shear_w)
    lame_w[...] = jnp.zeros_like(lame_w)
    for j in range(25):
        shear_w[8 * j : 8 * j + 5, :] = shear[5 * j : 5 * j + 5, :]
        lame_w[8 * j : 8 * j + 5, :] = lame[5 * j : 5 * j + 5, :]
    shear_w[...] = shear_w[...] * weight[...]
    lame_w[...] = lame_w[...] * weight[...]
    for s in range(2):
        for q in range(3):
            u[s, :, q * LANES : (q + 1) * LANES] = local_sum(gathered[2 * q + s])
            v[s, :, q * LANES : (q + 1) * LANES] = local_sum(gathered[COMPS + 2 * q + s])
    mass = local_sum(gathered[2 * COMPS])
    inverse[...] = 1.0 / jnp.where(mass > 0.0, mass, 1.0)

    def forces(i, carry):
        k, c = i // COMPS, i % COMPS
        force[i] = local_sum(gathered[FORCE_AT + 2 * STEPS * (c % 3) + 2 * k + c // 3])
        return carry

    lax.fori_loop(0, STEPS * COMPS, forces, 0)

    pl.semaphore_wait(barrier, 2 + 3 * jnp.minimum(lat, 1) + 3 * jnp.minimum(n_lat - 1 - lat, 1))

    ex40, _, _ = lane_parts((40, LANES))
    _, ey8, _ = lane_parts((8, LANES))
    slot8 = lax.broadcasted_iota(jnp.int32, (8, LANES), 1) // EZ
    corner_places = ((0, 0), (32, EYL - 1), (160, EYL * (EXB - 1)), (192, EYL * EXB - 1))

    def cols(c):
        return slice(c * LANES, (c + 1) * LANES)

    rows = (jnp.maximum(lat - 1, 0), jnp.minimum(lat + 1, n_lat - 1))

    def copy(src, dst, ss, rs, other, row):
        return pltpu.make_async_remote_copy(
            src_ref=src, dst_ref=dst, send_sem=ss, recv_sem=rs,
            device_id=(other, row), device_id_type=MESH,
        )

    def copies(j, s):
        x_copies = [
            copy(send_x.at[s, i], recv_x.at[j, i], sx.at[j, i], rx.at[j, i], (down, up)[i], lat)
            for i in range(2)
        ]
        y_copies = [
            copy(send_y.at[s, i], recv_y.at[j, i], sy.at[j, i], ry.at[j, i], blk, rows[i])
            for i in range(2)
        ]
        c_copies = [
            copy(send_c.at[s, i], recv_c.at[j, i], sc.at[j, i], rc.at[j, i], (down, up)[i // 2], rows[i % 2])
            for i in range(4)
        ]
        to_down = [y_copies[0], c_copies[0], c_copies[2]]
        to_up = [y_copies[1], c_copies[1], c_copies[3]]
        return x_copies, to_down, to_up

    def compute(j, s):
        k = j // 2
        high, low = parts(u[s])
        grads[...] = product(fwd_high[...], fwd_low[...], high, low)
        g = [[grads[d * ROWS : (d + 1) * ROWS, cols(q)] for q in range(3)] for d in range(3)]
        pressure = lame_w[...] * (g[0][0] + g[1][1] + g[2][2])
        for d in range(3):
            for q in range(d, 3):
                stress = shear_w[...] * (g[d][q] + g[q][d])
                if d == q:
                    stress = stress + pressure
                sh, sl = parts(stress)
                flux_high[d * ROWS : (d + 1) * ROWS, cols(q)] = sh
                flux_low[d * ROWS : (d + 1) * ROWS, cols(q)] = sl
                if d != q:
                    flux_high[q * ROWS : (q + 1) * ROWS, cols(d)] = sh
                    flux_low[q * ROWS : (q + 1) * ROWS, cols(d)] = sl
        t = [[grads[d * ROWS + 5 : d * ROWS + 6, cols(q)] for q in range(3)] for d in range(3)]
        third = (t[0][0] + t[1][1] + t[2][2]) / 3.0
        pieces = (
            t[0][0] - third,
            t[1][1] - third,
            0.5 * (t[0][1] + t[1][0]),
            0.5 * (t[0][2] + t[2][0]),
            0.5 * (t[1][2] + t[2][1]),
        )
        for m in range(5):
            integrals[j, m : m + 1, :] = pieces[m]
        balance[...] = product(bwd_high[...], bwd_low[...], flux_high[...], flux_low[...])
        for q in range(3):
            balance[:, cols(q)] = force[3 * j + q] - local_sum(balance[:, cols(q)])

        low0, low1 = balance[0:40, cols(0)], balance[0:40, cols(1)]
        top0, top1 = balance[160:200, cols(0)], balance[160:200, cols(1)]
        send_x[s, 0, :, cols(0)] = jnp.where(ex40 == 0, low0, pltpu.roll(low1, HALF_X, 1))
        send_x[s, 1, :, cols(0)] = jnp.where(ex40 == 1, top0, pltpu.roll(top1, HALF_X, 1))
        send_x[s, 0, :, cols(1)] = balance[0:40, cols(2)]
        send_x[s, 1, :, cols(1)] = pltpu.roll(balance[160:200, cols(2)], HALF_X, 1)
        for a in range(5):
            low_pack = balance[40 * a : 40 * a + 8, cols(0)]
            top_pack = pltpu.roll(balance[40 * a + 32 : 40 * a + 40, cols(0)], LANES - 3 * EZ, 1)
            for q in range(1, 3):
                low_face = pltpu.roll(balance[40 * a : 40 * a + 8, cols(q)], q * EZ, 1)
                top_face = pltpu.roll(
                    balance[40 * a + 32 : 40 * a + 40, cols(q)], LANES - (3 - q) * EZ, 1
                )
                low_pack = jnp.where(ey8 == q, low_face, low_pack)
                top_pack = jnp.where(ey8 == q, top_face, top_pack)
            send_y[s, 0, 8 * a : 8 * a + 8, :] = low_pack
            send_y[s, 1, 8 * a : 8 * a + 8, :] = top_pack
        for corner in range(4):
            r, home = corner_places[corner]
            pack = jnp.zeros((8, LANES), jnp.float32)
            for q in range(3):
                edge = balance[r : r + 8, cols(q)]
                shift = (q - home) * EZ % LANES
                if shift:
                    edge = pltpu.roll(edge, shift, 1)
                pack = jnp.where(slot8 == q, edge, pack)
            send_c[s, corner] = pack

        x_copies, to_down, to_up = copies(j, s)
        for one in x_copies:
            one.start()

        @pl.when(has_down)
        def _():
            for one in to_down:
                one.start()

        @pl.when(has_up)
        def _():
            for one in to_up:
                one.start()

        for q in range(3):
            speed = v[s, :, cols(q)] + balance[:, cols(q)] * inverse[...]
            v[s, :, cols(q)] = speed
            u[s, :, cols(q)] = u[s, :, cols(q)] + speed

    def finish(j, s):
        x_copies, to_down, to_up = copies(j, s)
        for one in x_copies:
            one.wait()

        @pl.when(has_down)
        def _():
            for one in to_down:
                one.wait_send()
            for one in to_up:
                one.wait_recv()

        @pl.when(has_up)
        def _():
            for one in to_up:
                one.wait_send()
            for one in to_down:
                one.wait_recv()

        def bump(r, size, q, extra):
            extra = extra * inverse[r : r + size, :]
            v[s, r : r + size, cols(q)] = v[s, r : r + size, cols(q)] + extra
            u[s, r : r + size, cols(q)] = u[s, r : r + size, cols(q)] + extra

        for q in range(3):
            from_up = recv_x[j, 0, :, cols(q // 2)]
            from_down = recv_x[j, 1, :, cols(q // 2)]
            if q == 0:
                from_down = pltpu.roll(from_down, HALF_X, 1)
            if q != 1:
                from_up = pltpu.roll(from_up, HALF_X, 1)
            bump(0, 40, q, jnp.where(ex40 == 0, from_down, 0.0))
            bump(160, 40, q, jnp.where(ex40 == 1, from_up, 0.0))
        for a in range(5):
            for q in range(3):
                fd = recv_y[j, 1, 8 * a : 8 * a + 8, :]
                fu = pltpu.roll(recv_y[j, 0, 8 * a : 8 * a + 8, :], (3 - q) * EZ, 1)
                if q:
                    fd = pltpu.roll(fd, LANES - q * EZ, 1)
                bump(40 * a, 8, q, jnp.where(ey8 == 0, fd, 0.0))
                bump(40 * a + 32, 8, q, jnp.where(ey8 == EYL - 1, fu, 0.0))
        for corner in range(4):
            r, home = corner_places[corner]
            pack = recv_c[j, 3 - corner]
            for q in range(3):
                shift = (home - q) * EZ % LANES
                edge = pltpu.roll(pack, shift, 1) if shift else pack
                bump(r, 8, q, jnp.where(slot8 == home, edge, 0.0))

    def half(j, carry):
        s = j % 2

        @pl.when(j >= 2)
        def _():
            finish(j - 2, s)

        @pl.when(j < 2 * STEPS)
        def _():
            compute(j, s)

        return carry

    lax.fori_loop(0, 2 * STEPS + 2, half, 0)
    for s in range(2):
        for q in range(3):
            at = 2 * q + s
            state[at * ROWS : (at + 1) * ROWS, :] = u[s, :, cols(q)]
            state[(COMPS + at) * ROWS : (COMPS + at + 1) * ROWS, :] = v[s, :, cols(q)]
    state[2 * COMPS * ROWS :, :] = jnp.zeros((4 * ROWS, LANES), jnp.float32)


def scatter_kernel(numbers, spectra, state, integrals, out_u, out_v, spectrum, table, stage):
    parts_of = lane_parts((16, LANES))

    def point(members, own, last):
        merged = None
        for p, row, move in members:
            block = state[pl.ds(row, 16, stride=ROWS), :]
            if shift_of(move):
                block = pltpu.roll(block, LANES - shift_of(move), 1)
            if merged is None:
                merged = block
            else:
                merged = jnp.where(chosen_lanes(last, move, parts_of), block, merged)
        stage[:, :16] = merged.T
        for p, row, move in members:
            for batch in in_batches(own, 16):
                lines = [stage[pl.ds(e - shift_of(move), 1), :] for e in batch]
                for e, line in zip(batch, lines):
                    table[pl.ds(numbers[p, e], 1), :] = line

    over_points(point)
    count = out_u.shape[2]

    def emit(at, width):
        block = table[pl.ds(at, LANES), :16].T
        for q in range(3):
            out_u[q, :, pl.ds(at, width)] = block[2 * q : 2 * q + 2, :width]
            out_v[q, :, pl.ds(at, width)] = block[COMPS + 2 * q : COMPS + 2 * q + 2, :width]

    def turn(i, carry):
        emit(pl.multiple_of(i * LANES, LANES), LANES)
        return carry

    lax.fori_loop(0, count // LANES, turn, 0)
    if count % LANES:
        emit(count // LANES * LANES, count % LANES)

    def frequency(f, carry):
        for part in range(2):
            for s in range(2):
                total = spectra[part, STEPS * f] * integrals[s, 0:5, :]
                for k in range(1, STEPS):
                    total = total + spectra[part, STEPS * f + k] * integrals[2 * k + s, 0:5, :]
                spectrum[part, f, :, s, :] = total
        return carry

    lax.fori_loop(0, NFREQ, frequency, 0)


def local(n_blk, n_lat, displacement, velocity, lumped_mass, shear, lame, sources, numbers, event_frequency):
    nodes = displacement.shape[2]
    padded = -(-nodes // LANES) * LANES
    omega = jnp.pi * (1.0 + jnp.arange(NFREQ, dtype=jnp.float32)) / (NFREQ + 1.0)
    onehot = (event_frequency[:, :, None] == jnp.arange(NFREQ, dtype=jnp.int32)[None, None, :])
    chosen = jnp.sum(onehot.astype(jnp.float32) * omega[None, None, :], axis=2)
    times = 1.0 + jnp.arange(STEPS, dtype=jnp.float32)
    pulse = jnp.cos(times[:, None, None] * chosen[None]).astype(jnp.bfloat16)
    phase = omega[:, None] * times[None, :]
    spectra = jnp.stack([jnp.cos(phase), -jnp.sin(phase)]).reshape(2, NFREQ * STEPS)
    force = jnp.einsum(
        "ce,eqn->qcn", pulse.reshape(STEPS * 2, -1), sources, preferred_element_type=jnp.float32
    )
    in_smem = pl.BlockSpec(memory_space=pltpu.SMEM)
    in_vmem = pl.BlockSpec(memory_space=VMEM)
    gathered = pl.pallas_call(
        gather_kernel,
        out_shape=jax.ShapeDtypeStruct((TABLE * ROWS, LANES), jnp.float32),
        in_specs=[in_smem] + [in_vmem] * 4,
        out_specs=in_vmem,
        scratch_shapes=[VMEM((padded, LANES), jnp.float32), VMEM((LANES, LANES), jnp.float32)],
        compiler_params=pltpu.CompilerParams(vmem_limit_bytes=LIMIT),
        name="gather_nodes",
    )(
        numbers, displacement.transpose(1, 0, 2), velocity.transpose(1, 0, 2), lumped_mass[None], force
    )
    forward, backward, weight = operators()
    wide = 3 * LANES
    f32, bf16 = jnp.float32, jnp.bfloat16
    state, integrals = pl.pallas_call(
        functools.partial(step_kernel, n_blk, n_lat),
        out_shape=(
            jax.ShapeDtypeStruct((16 * ROWS, LANES), f32),
            jax.ShapeDtypeStruct((2 * STEPS, 8, LANES), f32),
        ),
        in_specs=[in_vmem] * 8,
        out_specs=(in_vmem, in_vmem),
        scratch_shapes=[
            VMEM((2, ROWS, wide), f32),
            VMEM((2, ROWS, wide), f32),
            VMEM((STEPS * COMPS, ROWS, LANES), f32),
            VMEM((ROWS, LANES), f32),
            VMEM((ROWS, LANES), f32),
            VMEM((ROWS, LANES), f32),
            VMEM((3 * ROWS, wide), f32),
            VMEM((3 * ROWS, wide), bf16),
            VMEM((3 * ROWS, wide), bf16),
            VMEM((ROWS, wide), f32),
            VMEM((2, 2, 40, 2 * LANES), f32),
            VMEM((2, 2, 40, LANES), f32),
            VMEM((2, 4, 8, LANES), f32),
            VMEM((2 * STEPS, 2, 40, 2 * LANES), f32),
            VMEM((2 * STEPS, 2, 40, LANES), f32),
            VMEM((2 * STEPS, 4, 8, LANES), f32),
            pltpu.SemaphoreType.DMA((2 * STEPS, 2)),
            pltpu.SemaphoreType.DMA((2 * STEPS, 2)),
            pltpu.SemaphoreType.DMA((2 * STEPS, 2)),
            pltpu.SemaphoreType.DMA((2 * STEPS, 2)),
            pltpu.SemaphoreType.DMA((2 * STEPS, 4)),
            pltpu.SemaphoreType.DMA((2 * STEPS, 4)),
        ],
        compiler_params=pltpu.CompilerParams(
            vmem_limit_bytes=LIMIT, collective_id=0, has_side_effects=True
        ),
        name="time_steps",
    )(
        gathered.reshape(TABLE, ROWS, LANES), shear, lame, jnp.asarray(weight),
        *two_parts(forward), *two_parts(backward),
    )
    final_u, final_v, spectrum = pl.pallas_call(
        scatter_kernel,
        out_shape=(
            jax.ShapeDtypeStruct((3, 2, nodes), f32),
            jax.ShapeDtypeStruct((3, 2, nodes), f32),
            jax.ShapeDtypeStruct((2, NFREQ, 5, 2, LANES), f32),
        ),
        in_specs=[in_smem, in_smem, in_vmem, in_vmem],
        out_specs=(in_vmem,) * 3,
        scratch_shapes=[VMEM((padded, LANES), f32), VMEM((LANES, LANES), f32)],
        compiler_params=pltpu.CompilerParams(vmem_limit_bytes=LIMIT),
        name="scatter_nodes",
    )(numbers, spectra, state, integrals)
    return (
        final_u.transpose(1, 0, 2),
        final_v.transpose(1, 0, 2),
        spectrum.transpose(0, 1, 3, 2, 4),
    )


def solution(mesh):
    both = ("blk", "lat")
    return jax.shard_map(
        functools.partial(local, mesh.shape["blk"], mesh.shape["lat"]),
        mesh=mesh,
        in_specs=(
            P(None, None, both), P(None, None, both), P(both), P(None, both), P(None, both),
            P(None, None, both), P(None, both), P(),
        ),
        out_specs=(P(None, None, both), P(None, None, both), P(None, None, None, None, both)),
        check_vma=False,
    )
```
